512 devices in a mesh: tm: 8 (over z_lo), height: 64 (over z_hi, y, x, core).
Axes of the slice: x: 4, y: 4, z: 16 (z_hi: 2, z_lo: 8; z = z_hi * 8 + z_lo), core: 2. Of those that a mesh axis runs over, the one named last changes fastest.
Arguments:
- features: bfloat16 [96, 32, 256, 128], P(None, 'tm', 'height'), may hold values from -6 to 6
- first_gain: float32 [96], replicated, may hold values from 0.1 to 1.9
- first_weight: bfloat16 [96, 2592], replicated, may hold values from -0.125 to 0.125
- first_bias: float32 [96], replicated, may hold values from -3 to 3
- second_gain: float32 [96], replicated, may hold values from 0.1 to 1.9
- second_weight: bfloat16 [96, 2592], replicated, may hold values from -0.125 to 0.125
- second_bias: float32 [96], replicated, may hold values from -3 to 3
Outputs:
- encoded: bfloat16 [96, 32, 256, 128], P(None, 'tm', 'height')
The draws below stay inside these ranges and needn't reach their ends.
All inputs are finite; a program needn't handle non-finite values.
Results may differ from the reference program's by a relative error of at most 0.0036.
Values may be sent and summed in bfloat16 or wider, within the bound.
No kernel may reach another device: no remote copies, remote signals or barrier semaphores. Data moves between devices by JAX's collectives and lax.ppermute only.
A program may use at most 64 MiB of HBM per device.

```python
import jax
import jax.numpy as jnp
from jax import lax

C = 96
COLS = 128
FRAMES = 32
ROWS = 256


def block_scale(stream_key, shape, pieces, smallest, top_value):
    level = 1.0
    for position, shards_of in pieces:
        steps = jax.random.uniform(jax.random.fold_in(jax.random.fold_in(stream_key, 6), position), (shards_of,), jnp.float32, smallest / len(pieces), top_value / len(pieces))
        level = level * jnp.repeat(jnp.exp(steps), shape[position] // shards_of).reshape((-1,) + (1,) * (len(shape) - 1 - position))
    return level


def scatter_about(stream_key, shape, deviation, limit, shards=(), dtype=jnp.bfloat16):
    level = block_scale(stream_key, shape, shards, -0.22, 0.18) if shards else 1.0
    drawn = jax.random.normal(stream_key, shape, jnp.float32) * deviation * level
    return jnp.minimum(jnp.maximum(drawn, -limit), limit).astype(dtype)


def setup_inputs(seed: int = 0) -> dict:
    key_list = jax.random.split(jax.random.key(seed), 8)
    return {
        "features": scatter_about(key_list[0], (C, FRAMES, ROWS, COLS), 1.0, 6.0, ((1, 8), (2, 64))),
        "first_gain": jnp.clip(1.0 + 0.18 * jax.random.normal(key_list[1], (C,), jnp.float32), 0.1, 1.9),
        "first_weight": scatter_about(key_list[2], (C, 27 * C), (27 * C) ** -0.5, 0.125),
        "first_bias": scatter_about(key_list[3], (C,), 0.5, 3.0, (), jnp.float32),
        "second_gain": jnp.clip(1.0 + 0.18 * jax.random.normal(key_list[4], (C,), jnp.float32), 0.1, 1.9),
        "second_weight": scatter_about(key_list[5], (C, 27 * C), (27 * C) ** -0.5, 0.125),
        "second_bias": scatter_about(key_list[6], (C,), 0.5, 3.0, (), jnp.float32),
    }


def activate(values, gain_vector):
    mean_square = lax.optimization_barrier(jnp.mean(values * values, axis=0, keepdims=True))
    scaled = values * lax.rsqrt(mean_square + 1e-06) * gain_vector[:, None, None, None]
    return jax.nn.silu(scaled).astype(jnp.bfloat16)

def causal_conv(inputs, weight, bias_vector):
    kernel = weight.astype(jnp.float32).reshape(C, 3, 3, 3, C).transpose(0, 4, 1, 2, 3)
    result = lax.conv_general_dilated(inputs.astype(jnp.float32)[None], kernel, (1, 1, 1), ((2, 0), (1, 1), (1, 1)), dimension_numbers=('NCDHW', 'OIDHW', 'NCDHW'), precision=lax.Precision.HIGHEST)[0]
    return result + bias_vector.astype(jnp.float32)[:, None, None, None]

def reference(features, first_gain, first_weight, first_bias, second_gain, second_weight, second_bias):
    first_act = activate(features.astype(jnp.float32), first_gain)
    hidden = causal_conv(first_act, first_weight, first_bias)
    second_act = activate(hidden, second_gain)
    branch = causal_conv(second_act, second_weight, second_bias)
    return (features.astype(jnp.float32) + branch).astype(jnp.bfloat16)
```

```python
import functools

import jax
import jax.numpy as jnp
from jax import lax
from jax.experimental import pallas as pl
from jax.experimental.pallas import tpu as pltpu
from jax.sharding import PartitionSpec as P

C = 96
W = 128
TAPS = 9 * C
BF16 = jnp.bfloat16
F32 = jnp.float32
VMEM = pl.BlockSpec(memory_space=pltpu.VMEM)
PARAMS = pltpu.CompilerParams(vmem_limit_bytes=24 * 1024 * 1024)


def column(row):
    here = lax.broadcasted_iota(jnp.int32, (C, C), 0) == lax.broadcasted_iota(jnp.int32, (C, C), 1)
    return jnp.sum(jnp.where(here, row, 0.0), axis=1, keepdims=True)


def activation(values, gain):
    mean_square = jnp.sum(values * values, axis=0, keepdims=True) * (1.0 / C)
    scaled = values * lax.rsqrt(mean_square + 1e-06) * gain
    return scaled * (1.0 / (1.0 + jnp.exp(-scaled)))


def orientation():
    odd = lax.rem(lax.axis_index("height"), 2)
    return odd, 1 - 2 * odd


def natural(row, odd):
    return row + odd * (3 - 2 * row)


def first_act_kernel(features, gain_row, act, wide):
    odd, _ = orientation()
    gain = jnp.broadcast_to(column(gain_row[...]), (C, W))
    wide[...] = features[...].astype(F32)
    for frame in range(4):
        for row in range(4):
            values = wide[pl.ds(frame * 4 + row, C, stride=16), :]
            act[frame, natural(row, odd)] = activation(values, gain).astype(BF16)


def weight_kernel(first, second, first_bias, second_gain, second_bias, first_out, second_out, columns):
    for step, row in enumerate((first_bias, second_gain, second_bias)):
        columns[step] = jnp.broadcast_to(column(row[...]), (C, W))
    for source, target in ((first, first_out), (second, second_out)):
        for time_row in range(9):
            for tap in range(3):
                offset = (time_row * 3 + tap) * C
                target[tap * C : (tap + 1) * C, time_row * C : (time_row + 1) * C] = source[
                    :, offset : offset + C
                ]


def conv_pair(acts, weight, bias, frame, row, sign):
    columns = []
    for centre in (row, row + 1):
        blocks = [acts[frame + p, centre + sign * (q - 1)] for p in range(3) for q in range(3)]
        columns.append(jnp.concatenate(blocks, axis=0))
    stacked = jnp.concatenate(columns, axis=1)
    sums = jnp.dot(weight[...], stacked, preferred_element_type=F32)
    lane = lax.broadcasted_iota(jnp.int32, (C, W), 1)
    results = []
    for half in range(2):
        part = sums[:, half * W : (half + 1) * W]
        left = jnp.where(lane == 0, 0.0, pltpu.roll(part[:C], 1, 1))
        right = jnp.where(lane == W - 1, 0.0, pltpu.roll(part[2 * C :], W - 1, 1))
        results.append(part[C : 2 * C] + left + right + bias)
    return results


def near_kernel(
    own, earlier, even, first_weight, second_weight, columns,
    hidden_out, branch_out, acts, hidden,
):
    _, sign = orientation()
    started = lax.axis_index("tm") > 0
    for frame in range(4):
        acts[frame, 0:4] = earlier[frame]
        acts[frame + 4, 0:4] = own[frame]
    for frame in range(8):
        acts[frame, 4] = even[frame, 1]
        acts[frame, 5] = even[frame, 0]
    bias, gain, last_bias = columns[0], columns[1], columns[2]

    @pl.loop(0, 6)
    def _(frame):
        inside = jnp.logical_or(started, frame >= 2)
        for row in (1, 3):
            pair = conv_pair(acts, first_weight, bias, frame, row, sign)
            for step, values in enumerate(pair):
                result = jnp.where(inside, activation(values, gain), 0.0).astype(BF16)
                hidden[frame, row - 1 + step] = result
                if row == 1:
                    hidden_out[frame, step] = result

    @pl.loop(0, 4)
    def _(frame):
        pair = conv_pair(hidden, second_weight, last_bias, frame, 1, sign)
        for step, values in enumerate(pair):
            branch_out[frame, step] = values


def far_kernel(
    features, own, earlier, far, far_earlier, near_hidden, near_branch,
    first_weight, second_weight, columns,
    encoded, acts, hidden, total,
):
    odd, sign = orientation()
    started = lax.axis_index("tm") > 0
    height = lax.axis_index("height")
    bordered = jnp.logical_or(height == 0, height == lax.axis_size("height") - 1)
    for frame in range(4):
        for step in range(2):
            acts[frame, 1 - step] = far_earlier[frame, step]
            acts[frame + 4, 1 - step] = far[frame, step]
            acts[frame, 2 + step] = earlier[frame, step]
            acts[frame + 4, 2 + step] = own[frame, step]
    for frame in range(6):
        hidden[frame, 2:4] = near_hidden[frame]
    bias, gain, last_bias = columns[0], columns[1], columns[2]

    @pl.loop(0, 6)
    def _(frame):
        inside = jnp.logical_or(started, frame >= 2)
        pair = conv_pair(acts, first_weight, bias, frame, 1, sign)
        for step, values in enumerate(pair):
            keep = jnp.logical_and(inside, jnp.logical_not(bordered)) if step == 0 else inside
            hidden[frame, step] = jnp.where(keep, activation(values, gain), 0.0).astype(BF16)

    @pl.loop(0, 4)
    def _(frame):
        pair = conv_pair(hidden, second_weight, last_bias, frame, 1, sign)
        for step, values in enumerate(pair):
            total[pl.ds(frame * 4 + natural(step, odd), C, stride=16), :] = values
            total[pl.ds(frame * 4 + natural(step + 2, odd), C, stride=16), :] = near_branch[frame, step]

    encoded[...] = (features[...].astype(F32) + total[...]).astype(BF16)


def shape(*dims, dtype=BF16):
    return jax.ShapeDtypeStruct(dims, dtype)


def call(kernel, out_shape, scratch, inputs, **kwargs):
    many = isinstance(out_shape, (list, tuple))
    return pl.pallas_call(
        kernel,
        out_shape=out_shape,
        in_specs=[VMEM] * len(inputs),
        out_specs=[VMEM] * len(out_shape) if many else VMEM,
        scratch_shapes=scratch,
        compiler_params=PARAMS,
        **kwargs,
    )(*inputs)


def held(array, flops):
    return pl.pallas_call(
        lambda source, target: None,
        out_shape=jax.ShapeDtypeStruct(array.shape, array.dtype),
        in_specs=[pl.BlockSpec(memory_space=pl.ANY)],
        out_specs=pl.BlockSpec(memory_space=pl.ANY),
        input_output_aliases={0: 0},
        compiler_params=pltpu.CompilerParams(vmem_limit_bytes=1 << 20),
        cost_estimate=pl.CostEstimate(flops=flops, bytes_accessed=0, transcendentals=0),
    )(array)


def swap_pairs(first, count):
    edges = [(i, i + 1) for i in range(first, count - 1, 2)]
    return edges + [(b, a) for a, b in edges]


def local(features, first_gain, first_weight, first_bias, second_gain, second_weight, second_bias):
    height, times = lax.axis_size("height"), lax.axis_size("tm")
    later = [(i, i + 1) for i in range(times - 1)]
    flat = features.reshape(C * 16, W)
    rows = [v.reshape(1, C) for v in (first_bias, second_gain, second_bias)]

    act = call(
        first_act_kernel, shape(4, 4, C, W), [pltpu.VMEM((C * 16, W), F32)],
        (flat, first_gain.reshape(1, C)),
    )
    far = lax.ppermute(act[:, 0:2], "height", swap_pairs(1, height))
    prepared = call(
        weight_kernel,
        [shape(3 * C, TAPS), shape(3 * C, TAPS), shape(3, C, W, dtype=F32)], [],
        (first_weight, second_weight, *rows),
        cost_estimate=pl.CostEstimate(flops=1 << 35, bytes_accessed=1 << 21, transcendentals=0),
    )
    earlier = lax.ppermute(act, "tm", later)
    both = jnp.concatenate([earlier[:, 2:4], act[:, 2:4]], axis=0)
    both, prepared = lax.optimization_barrier((both, prepared))
    even = lax.ppermute(both, "height", swap_pairs(0, height))
    far = held(far, 1 << 33)
    far, even = lax.optimization_barrier((far, even))
    far_earlier = lax.ppermute(far, "tm", later)
    near_hidden, near_branch = call(
        near_kernel, [shape(6, 2, C, W), shape(4, 2, C, W, dtype=F32)],
        [pltpu.VMEM((8, 6, C, W), BF16), pltpu.VMEM((6, 4, C, W), BF16)],
        (act, earlier, even, *prepared),
        cost_estimate=pl.CostEstimate(flops=32 * W * C * TAPS * 6, bytes_accessed=1 << 21, transcendentals=0),
    )
    encoded = call(
        far_kernel, shape(C * 16, W),
        [pltpu.VMEM((8, 4, C, W), BF16), pltpu.VMEM((6, 4, C, W), BF16), pltpu.VMEM((C * 16, W), F32)],
        (flat, act, earlier, far, far_earlier, near_hidden, near_branch, *prepared),
        cost_estimate=pl.CostEstimate(flops=20 * W * C * TAPS * 6, bytes_accessed=1 << 21, transcendentals=0),
    )
    return encoded.reshape(features.shape)


def solution(mesh):
    return jax.shard_map(
        local,
        mesh=mesh,
        in_specs=(P(None, "tm", "height", None), P(), P(), P(), P(), P(), P()),
        out_specs=P(None, "tm", "height", None),
        check_vma=False,
    )
```

```python
import functools

import jax
import jax.numpy as jnp
from jax import lax
from jax.experimental import pallas as pl
from jax.experimental.pallas import tpu as pltpu
from jax.sharding import PartitionSpec as P

C = 96
W = 128
TAPS = 9 * C
BF16 = jnp.bfloat16
F32 = jnp.float32
VMEM = pl.BlockSpec(memory_space=pltpu.VMEM)
PARAMS = pltpu.CompilerParams(vmem_limit_bytes=24 * 1024 * 1024)


def column(row):
    here = lax.broadcasted_iota(jnp.int32, (C, C), 0) == lax.broadcasted_iota(jnp.int32, (C, C), 1)
    return jnp.sum(jnp.where(here, row, 0.0), axis=1, keepdims=True)


def activation(values, gain):
    mean_square = jnp.sum(values * values, axis=0, keepdims=True) * (1.0 / C)
    scaled = values * lax.rsqrt(mean_square + 1e-06) * gain
    return scaled * (1.0 / (1.0 + jnp.exp(-scaled)))


def natural(row):
    return row + lax.rem(lax.axis_index("height"), 2) * (3 - 2 * row)


def first_act_kernel(features_in, gain_in, edge, act, sent, features, gain_row, wide, arrived):
    copies = [
        pltpu.make_async_copy(features_in, features, arrived.at[0]),
        pltpu.make_async_copy(gain_in, gain_row, arrived.at[1]),
    ]
    for copy in copies:
        copy.start()
    for copy in copies:
        copy.wait()
    gain = jnp.broadcast_to(column(gain_row[...]), (C, W))
    wide[...] = features[...].astype(F32)
    for frame in range(4):
        for row in range(4):
            values = wide[pl.ds(frame * 4 + row, C, stride=16), :]
            result = activation(values, gain).astype(BF16)
            act[frame, natural(row)] = result
    edge[...] = act[:, 0:2]
    sent[...] = act[...]


def weight_kernel(first, second, first_bias, second_gain, second_bias, *targets):
    columns = targets[-1]
    for step, row in enumerate((first_bias, second_gain, second_bias)):
        columns[step] = jnp.broadcast_to(column(row[...]), (C, W))
    reversed_rows = lax.rem(lax.axis_index("height"), 2) == 1
    for source, (whole, late, last) in ((first, targets[0:3]), (second, targets[3:6])):
        for row_tap in range(3):
            for time_tap in range(3):
                place = (row_tap * 3 + time_tap) * C
                for tap in range(3):
                    offset = ((time_tap * 3 + row_tap) * 3 + tap) * C
                    mirrored = ((time_tap * 3 + 2 - row_tap) * 3 + tap) * C
                    block = jnp.where(
                        reversed_rows, source[:, mirrored : mirrored + C], source[:, offset : offset + C]
                    )
                    lines = slice(tap * C, (tap + 1) * C)
                    whole[lines, place : place + C] = block
                    if row_tap >= 1:
                        late[lines, place - 3 * C : place - 2 * C] = block
                    if row_tap == 2:
                        last[lines, place - 6 * C : place - 5 * C] = block


def products(weight, left, right):
    stacked = jnp.concatenate([jnp.concatenate(left, axis=0), jnp.concatenate(right, axis=0)], axis=1)
    sums = jnp.dot(weight, stacked, preferred_element_type=F32)
    lane = lax.broadcasted_iota(jnp.int32, (C, W), 1)
    results = []
    for half in range(2):
        part = sums[:, half * W : (half + 1) * W]
        before = jnp.where(lane == 0, 0.0, pltpu.roll(part[:C], 1, 1))
        after = jnp.where(lane == W - 1, 0.0, pltpu.roll(part[2 * C :], W - 1, 1))
        results.append(part[C : 2 * C] + before + after)
    return results


def window(cell, frame, rows):
    return [cell(frame + step, row) for row in rows for step in range(3)]


def borders():
    height = lax.axis_index("height")
    outer = jnp.logical_or(height == 0, height == lax.axis_size("height") - 1)
    return lax.axis_index("tm") > 0, jnp.logical_not(outer)


def near_kernel(
    own, earlier, even, far, first_weight, first_late, first_last, second_weight, second_late, second_last, columns,
    branch_out, far_hidden, first_part, branch_part, hidden,
):
    started, joined = borders()
    bias, gain, last_bias = columns[0], columns[1], columns[2]

    def act(frame, row):
        if row < 0:
            return far[frame - 4, -1 - row]
        if row > 3:
            return even[frame, 5 - row]
        return earlier[frame, row] if frame < 4 else own[frame - 4, row]

    def inner(frame, row):
        return hidden[frame, row - 1]

    for frame in range(6):
        for row in (1, 3):
            pair = products(
                first_weight[...], window(act, frame, range(row - 1, row + 2)), window(act, frame, range(row, row + 3))
            )
            for step, sums in enumerate(pair):
                result = activation(sums + bias, gain)
                if frame < 2:
                    result = jnp.where(started, result, 0.0)
                hidden[frame, row - 1 + step] = result.astype(BF16)
    for frame in range(4):
        pair = products(
            second_weight[...], window(inner, frame, range(1, 4)), window(inner, frame, range(2, 5))
        )
        for step, sums in enumerate(pair):
            branch_out[frame, step] = sums + last_bias

    for frame in (4, 5):
        pair = products(first_weight[...], window(act, frame, (-2, -1, 0)), window(act, frame, (-1, 0, 1)))
        for step, sums in enumerate(pair):
            result = activation(sums + bias, gain)
            if step == 0:
                result = jnp.where(joined, result, 0.0)
            far_hidden[frame - 4, step] = result.astype(BF16)
    for frame in (0, 2):
        for part, cell, base, weights, row in (
            (first_part, act, bias, (first_last, first_late), 0),
            (branch_part, inner, last_bias, (second_last, second_late), 1),
        ):
            for step, weight in enumerate(weights):
                rows = (row,) if step == 0 else (row, row + 1)
                pair = products(weight[...], window(cell, frame, rows), window(cell, frame + 1, rows))
                for later, sums in enumerate(pair):
                    part[frame + later, step] = sums + base


def far_kernel(
    features, far, far_earlier, far_hidden, near_branch, first_part, branch_part, first_weight, second_weight, columns,
    encoded, hidden, total,
):
    started, joined = borders()
    gain = columns[1]

    def act(frame, row):
        return far_earlier[frame, -1 - row] if frame < 4 else far[frame - 4, -1 - row]

    def outer(frame, row):
        return hidden[frame, row + 1] if frame < 4 else far_hidden[frame - 4, row + 1]

    for frame in (0, 2):
        for step, rows in ((0, (-2, -1)), (1, (-1,))):
            weight = first_weight[:, : len(rows) * 3 * C]
            pair = products(weight, window(act, frame, rows), window(act, frame + 1, rows))
            for later, sums in enumerate(pair):
                result = activation(sums + first_part[frame + later, step], gain)
                keep = None
                if frame == 0:
                    keep = jnp.logical_and(started, joined) if step == 0 else started
                elif step == 0:
                    keep = joined
                if keep is not None:
                    result = jnp.where(keep, result, 0.0)
                hidden[frame + later, step] = result.astype(BF16)
    for frame in range(4):
        for step in range(2):
            total[pl.ds(frame * 4 + natural(step + 2), C, stride=16), :] = near_branch[frame, step]
    for frame in (0, 2):
        for step, rows in ((0, (-1, 0)), (1, (0,))):
            weight = second_weight[:, : len(rows) * 3 * C]
            pair = products(weight, window(outer, frame, rows), window(outer, frame + 1, rows))
            for later, sums in enumerate(pair):
                place = (frame + later) * 4 + natural(step)
                total[pl.ds(place, C, stride=16), :] = sums + branch_part[frame + later, step]

    encoded[...] = (features[...].astype(F32) + total[...]).astype(BF16)


def shape(*dims, dtype=BF16):
    return jax.ShapeDtypeStruct(dims, dtype)


def call(kernel, out_shape, scratch, inputs, **kwargs):
    many = isinstance(out_shape, (list, tuple))
    return pl.pallas_call(
        kernel,
        out_shape=out_shape,
        in_specs=[VMEM] * len(inputs),
        out_specs=[VMEM] * len(out_shape) if many else VMEM,
        scratch_shapes=scratch,
        compiler_params=PARAMS,
        **kwargs,
    )(*inputs)


def held(array, flops):
    return pl.pallas_call(
        lambda source, target: None,
        out_shape=jax.ShapeDtypeStruct(array.shape, array.dtype),
        in_specs=[pl.BlockSpec(memory_space=pl.ANY)],
        out_specs=pl.BlockSpec(memory_space=pl.ANY),
        input_output_aliases={0: 0},
        compiler_params=pltpu.CompilerParams(vmem_limit_bytes=1 << 20),
        cost_estimate=pl.CostEstimate(flops=flops, bytes_accessed=0, transcendentals=0),
    )(array)


def swap_pairs(first, count):
    edges = [(i, i + 1) for i in range(first, count - 1, 2)]
    return edges + [(b, a) for a, b in edges]


def local(features, first_gain, first_weight, first_bias, second_gain, second_weight, second_bias):
    height, times = lax.axis_size("height"), lax.axis_size("tm")
    later = [(i, i + 1) for i in range(times - 1)]
    flat = features.reshape(C * 16, W)
    rows = [v.reshape(1, C) for v in (first_bias, second_gain, second_bias)]

    edge, act, sent = pl.pallas_call(
        first_act_kernel,
        out_shape=[shape(4, 2, C, W), shape(4, 4, C, W), shape(4, 4, C, W)],
        in_specs=[pl.BlockSpec(memory_space=pltpu.HBM)] * 2,
        out_specs=[VMEM] * 3,
        scratch_shapes=[
            pltpu.VMEM((C * 16, W), BF16), pltpu.VMEM((1, C), F32), pltpu.VMEM((C * 16, W), F32),
            pltpu.SemaphoreType.DMA((2,)),
        ],
        compiler_params=PARAMS,
    )(*(pltpu.with_memory_space_constraint(v, pltpu.HBM) for v in (flat, first_gain.reshape(1, C))))
    far = lax.ppermute(edge, "height", swap_pairs(1, height))
    prepared = call(
        weight_kernel,
        [shape(3 * C, width * C) for width in (9, 6, 3)] * 2 + [shape(3, C, W, dtype=F32)], [],
        (first_weight, second_weight, *rows),
        cost_estimate=pl.CostEstimate(flops=1 << 35, bytes_accessed=1 << 21, transcendentals=0),
    )
    earlier = lax.ppermute(held(sent, 1 << 33), "tm", later)
    both = jnp.concatenate([earlier[:, 2:4], act[:, 2:4]], axis=0)
    both, prepared = lax.optimization_barrier((both, prepared))
    even = lax.ppermute(both, "height", swap_pairs(0, height))
    far = held(far, 1 << 33)
    far_earlier = lax.ppermute(far, "tm", later)
    near_branch, far_hidden, first_part, branch_part = call(
        near_kernel,
        [shape(4, 2, C, W, dtype=F32), shape(2, 2, C, W), shape(4, 2, C, W, dtype=F32), shape(4, 2, C, W, dtype=F32)],
        [pltpu.VMEM((6, 4, C, W), BF16)],
        (act, earlier, even, far, *prepared),
        cost_estimate=pl.CostEstimate(flops=40 * W * C * TAPS * 6, bytes_accessed=1 << 21, transcendentals=0),
    )
    encoded = call(
        far_kernel, shape(C * 16, W),
        [pltpu.VMEM((4, 2, C, W), BF16), pltpu.VMEM((C * 16, W), F32)],
        (flat, far, far_earlier, far_hidden, near_branch, first_part, branch_part, prepared[0], prepared[3], prepared[6]),
        cost_estimate=pl.CostEstimate(flops=8 * W * C * TAPS * 6, bytes_accessed=1 << 21, transcendentals=0),
    )
    return encoded.reshape(features.shape)


def solution(mesh):
    return jax.shard_map(
        local,
        mesh=mesh,
        in_specs=(P(None, "tm", "height", None), P(), P(), P(), P(), P(), P()),
        out_specs=P(None, "tm", "height", None),
        check_vma=False,
    )
```

```python
import functools

import jax
import jax.numpy as jnp
from jax import lax
from jax.experimental import pallas as pl
from jax.experimental.pallas import tpu as pltpu
from jax.sharding import PartitionSpec as P

C = 96
W = 128
TAPS = 9 * C
TURNS = {1: 1, 3: 1, 6: 1, 4: 2}
BF16 = jnp.bfloat16
F32 = jnp.float32
VMEM = pl.BlockSpec(memory_space=pltpu.VMEM)
PARAMS = pltpu.CompilerParams(vmem_limit_bytes=24 * 1024 * 1024)


def column(row):
    here = lax.broadcasted_iota(jnp.int32, (C, C), 0) == lax.broadcasted_iota(jnp.int32, (C, C), 1)
    return jnp.sum(jnp.where(here, row, 0.0), axis=1, keepdims=True)


def activation(values, gain):
    mean_square = jnp.sum(values * values, axis=0, keepdims=True) * (1.0 / C)
    scaled = values * lax.rsqrt(mean_square + 1e-06) * gain
    return scaled * (1.0 / (1.0 + jnp.exp(-scaled)))


def natural(row):
    return row + lax.rem(lax.axis_index("height"), 2) * (3 - 2 * row)


def first_act_kernel(features_in, gain_in, act, features, gain_row, wide, arrived):
    copies = [
        pltpu.make_async_copy(features_in, features, arrived.at[0]),
        pltpu.make_async_copy(gain_in, gain_row, arrived.at[1]),
    ]
    for copy in copies:
        copy.start()
    for copy in copies:
        copy.wait()
    gain = jnp.broadcast_to(column(gain_row[...]), (C, W))
    wide[...] = features[...].astype(F32)
    for frame in range(4):
        for row in range(4):
            values = wide[pl.ds(frame * 4 + row, C, stride=16), :]
            result = activation(values, gain).astype(BF16)
            act[frame, natural(row)] = result


def weight_kernel(first, second, first_bias, second_gain, second_bias, *targets):
    columns = targets[-1]
    for step, row in enumerate((first_bias, second_gain, second_bias)):
        columns[step] = jnp.broadcast_to(column(row[...]), (C, W))
    reversed_rows = lax.rem(lax.axis_index("height"), 2) == 1

    def arrange(mirrored):
        for source, (whole, late, last) in ((first, targets[0:3]), (second, targets[3:6])):
            for row_tap in range(3):
                for time_tap in range(3):
                    place = (row_tap * 3 + time_tap) * C
                    source_row = 2 - row_tap if mirrored else row_tap
                    for tap in range(3):
                        offset = ((time_tap * 3 + source_row) * 3 + tap) * C
                        block = source[:, offset : offset + C]
                        lines = slice(tap * C, (tap + 1) * C)
                        whole[lines, place : place + C] = block
                        if row_tap >= 1:
                            late[lines, place - 3 * C : place - 2 * C] = block
                        if row_tap == 2:
                            last[lines, place - 6 * C : place - 5 * C] = block

    pl.when(reversed_rows)(lambda: arrange(True))
    pl.when(jnp.logical_not(reversed_rows))(lambda: arrange(False))


def products(weight, left, right):
    stacked = jnp.concatenate([jnp.concatenate(left, axis=0), jnp.concatenate(right, axis=0)], axis=1)
    sums = jnp.dot(weight, stacked, preferred_element_type=F32)
    lane = lax.broadcasted_iota(jnp.int32, (C, W), 1)
    results = []
    for half in range(2):
        part = sums[:, half * W : (half + 1) * W]
        before = jnp.where(lane == 0, 0.0, pltpu.roll(part[:C], 1, 1))
        after = jnp.where(lane == W - 1, 0.0, pltpu.roll(part[2 * C :], W - 1, 1))
        results.append(part[C : 2 * C] + before + after)
    return results


def window(cell, frame, rows):
    return [cell(frame + step, row) for row in rows for step in range(3)]


def borders():
    height = lax.axis_index("height")
    outer = jnp.logical_or(height == 0, height == lax.axis_size("height") - 1)
    return lax.axis_index("tm") > 0, jnp.logical_not(outer)


def near_kernel(own, earlier, even, first_weight, second_weight, columns, near_hidden, branch_out, hidden):
    started, _ = borders()
    bias, gain, last_bias = columns[0], columns[1], columns[2]
    partner = 1 - lax.rem(lax.axis_index("height"), 2)

    def act(frame, row):
        if row > 3:
            return even[partner, frame, 5 - row]
        return earlier[frame, row] if frame < 4 else own[frame - 4, row]

    def inner(frame, row):
        return hidden[frame, row - 1]

    for frame in range(6):
        for row in (1, 3):
            pair = products(
                first_weight[...], window(act, frame, range(row - 1, row + 2)), window(act, frame, range(row, row + 3))
            )
            for step, sums in enumerate(pair):
                result = activation(sums + bias, gain)
                if frame < 2:
                    result = jnp.where(started, result, 0.0)
                hidden[frame, row - 1 + step] = result.astype(BF16)
                if row == 1:
                    near_hidden[frame, step] = result.astype(BF16)
    for frame in range(4):
        pair = products(
            second_weight[...], window(inner, frame, range(1, 4)), window(inner, frame, range(2, 5))
        )
        for step, sums in enumerate(pair):
            branch_out[frame, step] = sums + last_bias


def partial_kernel(
    own, earlier, far, near_hidden, first_weight, first_late, first_last, second_late, second_last, columns, _,
    far_hidden, first_part, branch_part,
):
    _, joined = borders()
    bias, gain, last_bias = columns[0], columns[1], columns[2]

    def act(frame, row):
        if row < 0:
            return far[frame - 4, -1 - row]
        return earlier[frame, row] if frame < 4 else own[frame - 4, row]

    def inner(frame, row):
        return near_hidden[frame, row - 1]

    for frame in (4, 5):
        pair = products(first_weight[...], window(act, frame, (-2, -1, 0)), window(act, frame, (-1, 0, 1)))
        for step, sums in enumerate(pair):
            result = activation(sums + bias, gain)
            if step == 0:
                result = jnp.where(joined, result, 0.0)
            far_hidden[frame - 4, step] = result.astype(BF16)
    for frame in (0, 2):
        for part, cell, base, weights, row in (
            (first_part, act, bias, (first_last, first_late), 0),
            (branch_part, inner, last_bias, (second_last, second_late), 1),
        ):
            for step, weight in enumerate(weights):
                rows = (row,) if step == 0 else (row, row + 1)
                pair = products(weight[...], window(cell, frame, rows), window(cell, frame + 1, rows))
                for later, sums in enumerate(pair):
                    part[frame + later, step] = sums + base


def far_kernel(
    features, far, corner, second_corner, third_corner, far_hidden, near_branch, first_part, branch_part, first_weight, second_weight, columns,
    encoded, hidden, total,
):
    started, joined = borders()
    gain = columns[1]

    def act(frame, row):
        if frame < 4:
            return corner[frame, -1 - row] + second_corner[frame, -1 - row] + third_corner[frame, -1 - row]
        return far[frame - 4, -1 - row]

    def outer(frame, row):
        return hidden[frame, row + 1] if frame < 4 else far_hidden[frame - 4, row + 1]

    for frame in (0, 2):
        for step, rows in ((0, (-2, -1)), (1, (-1,))):
            weight = first_weight[:, : len(rows) * 3 * C]
            pair = products(weight, window(act, frame, rows), window(act, frame + 1, rows))
            for later, sums in enumerate(pair):
                result = activation(sums + first_part[frame + later, step], gain)
                keep = None
                if frame == 0:
                    keep = jnp.logical_and(started, joined) if step == 0 else started
                elif step == 0:
                    keep = joined
                if keep is not None:
                    result = jnp.where(keep, result, 0.0)
                hidden[frame + later, step] = result.astype(BF16)
    for frame in range(4):
        for step in range(2):
            total[pl.ds(frame * 4 + natural(step + 2), C, stride=16), :] = near_branch[frame, step]
    for frame in (0, 2):
        for step, rows in ((0, (-1, 0)), (1, (0,))):
            weight = second_weight[:, : len(rows) * 3 * C]
            pair = products(weight, window(outer, frame, rows), window(outer, frame + 1, rows))
            for later, sums in enumerate(pair):
                place = (frame + later) * 4 + natural(step)
                total[pl.ds(place, C, stride=16), :] = sums + branch_part[frame + later, step]

    encoded[...] = (features[...].astype(F32) + total[...]).astype(BF16)


def shape(*dims, dtype=BF16):
    return jax.ShapeDtypeStruct(dims, dtype)


def call(kernel, out_shape, scratch, inputs, **kwargs):
    many = isinstance(out_shape, (list, tuple))
    return pl.pallas_call(
        kernel,
        out_shape=out_shape,
        in_specs=[VMEM] * len(inputs),
        out_specs=[VMEM] * len(out_shape) if many else VMEM,
        scratch_shapes=scratch,
        compiler_params=PARAMS,
        **kwargs,
    )(*inputs)


def held(array, flops, *others):
    return pl.pallas_call(
        lambda *refs: None,
        out_shape=shape(*array.shape),
        in_specs=[pl.BlockSpec(memory_space=pl.ANY)] * (1 + len(others)),
        out_specs=pl.BlockSpec(memory_space=pl.ANY),
        input_output_aliases={0: 0},
        compiler_params=pltpu.CompilerParams(vmem_limit_bytes=1 << 20),
        cost_estimate=pl.CostEstimate(flops=flops, bytes_accessed=0, transcendentals=0),
    )(array, *others)


def swap_pairs(first, count):
    edges = [(i, i + 1) for i in range(first, count - 1, 2)]
    return edges + [(b, a) for a, b in edges]


def routes(times, height):
    middle = (height // 2 - 1, height // 2)
    crossing, corner = [[], [], []], [[], [], []]
    for time in range(times):
        for a, b in swap_pairs(1, height):
            turn = TURNS.get(time, 0) if a in middle and b in middle else 0
            crossing[turn].append((time * height + a, time * height + b))
        for place in range(height):
            turn = TURNS.get(time, 0) if place in middle else 0
            if time + 1 < times:
                corner[turn].append((time * height + place, (time + 1) * height + place))
    return crossing, corner


def local(features, first_gain, first_weight, first_bias, second_gain, second_weight, second_bias):
    height, times = lax.axis_size("height"), lax.axis_size("tm")
    later = [(i, i + 1) for i in range(times - 1)]
    flat = features.reshape(C * 16, W)
    rows = [v.reshape(1, C) for v in (first_bias, second_gain, second_bias)]

    act = pl.pallas_call(
        first_act_kernel,
        out_shape=shape(4, 4, C, W),
        in_specs=[pl.BlockSpec(memory_space=pltpu.HBM)] * 2,
        out_specs=VMEM,
        scratch_shapes=[
            pltpu.VMEM((C * 16, W), BF16), pltpu.VMEM((1, C), F32), pltpu.VMEM((C * 16, W), F32),
            pltpu.SemaphoreType.DMA((2,)),
        ],
        compiler_params=PARAMS,
    )(*(pltpu.with_memory_space_constraint(v, pltpu.HBM) for v in (flat, first_gain.reshape(1, C))))
    edge = act[:, 0:2]
    crossing, corner = routes(times, height)
    fars = [lax.ppermute(edge, ("tm", "height"), pairs) for pairs in crossing]
    prepared = call(
        weight_kernel,
        [shape(3 * C, width * C) for width in (9, 6, 3)] * 2 + [shape(3, C, W, dtype=F32)], [],
        (first_weight, second_weight, *rows),
        cost_estimate=pl.CostEstimate(flops=1 << 27, bytes_accessed=1 << 21, transcendentals=0),
    )
    first, first_late, first_last, second, second_late, second_last, columns = prepared
    earlier = lax.ppermute(act, "tm", later)
    both = jnp.concatenate([earlier[:, 2:4], act[:, 2:4]], axis=0)
    even = lax.all_gather(both, "height", axis_index_groups=[[i, i + 1] for i in range(0, height, 2)])
    near_hidden, near_branch = call(
        near_kernel, [shape(6, 2, C, W), shape(4, 2, C, W, dtype=F32)], [pltpu.VMEM((6, 4, C, W), BF16)],
        (act, earlier, even, first, second, columns),
        cost_estimate=pl.CostEstimate(flops=1 << 20, bytes_accessed=1 << 10, transcendentals=0),
    )
    fars = [held(far, 1 << 33, near_hidden) for far in fars]
    corners = [lax.ppermute(far, ("tm", "height"), pairs) for far, pairs in zip(fars, corner)]
    far = fars[0] + fars[1] + fars[2]
    far_hidden, first_part, branch_part = call(
        partial_kernel,
        [shape(2, 2, C, W), shape(4, 2, C, W, dtype=F32), shape(4, 2, C, W, dtype=F32)], [],
        (act, earlier, far, near_hidden, first, first_late, first_last, second_late, second_last, columns, corners[0]),
        cost_estimate=pl.CostEstimate(flops=1 << 30, bytes_accessed=1 << 21, transcendentals=0),
    )
    encoded = call(
        far_kernel, shape(C * 16, W),
        [pltpu.VMEM((4, 2, C, W), BF16), pltpu.VMEM((C * 16, W), F32)],
        (flat, far, *corners, far_hidden, near_branch, first_part, branch_part, first, second, columns),
        cost_estimate=pl.CostEstimate(flops=8 * W * C * TAPS * 6, bytes_accessed=1 << 21, transcendentals=0),
    )
    return encoded.reshape(features.shape)


def solution(mesh):
    return jax.shard_map(
        local,
        mesh=mesh,
        in_specs=(P(None, "tm", "height", None), P(), P(), P(), P(), P(), P()),
        out_specs=P(None, "tm", "height", None),
        check_vma=False,
    )
```

```python
import functools

import jax
import jax.numpy as jnp
from jax import lax
from jax.experimental import pallas as pl
from jax.experimental.pallas import tpu as pltpu
from jax.sharding import PartitionSpec as P

C = 96
W = 128
TAPS = 9 * C
TURNS = {1: 1, 3: 1, 6: 1, 4: 2}
BF16 = jnp.bfloat16
F32 = jnp.float32
VMEM = pl.BlockSpec(memory_space=pltpu.VMEM)
PARAMS = pltpu.CompilerParams(vmem_limit_bytes=24 * 1024 * 1024)


def column(row):
    here = lax.broadcasted_iota(jnp.int32, (C, C), 0) == lax.broadcasted_iota(jnp.int32, (C, C), 1)
    return jnp.sum(jnp.where(here, row, 0.0), axis=1, keepdims=True)


def activation(values, gain):
    mean_square = jnp.sum(values * values, axis=0, keepdims=True) * (1.0 / C)
    scaled = values * lax.rsqrt(mean_square + 1e-06) * gain
    return scaled * (1.0 / (1.0 + jnp.exp(-scaled)))


def natural(row):
    return row + lax.rem(lax.axis_index("height"), 2) * (3 - 2 * row)


def first_act_kernel(features_in, gain_in, act, features, gain_row, wide, arrived):
    copies = [
        pltpu.make_async_copy(features_in, features, arrived.at[0]),
        pltpu.make_async_copy(gain_in, gain_row, arrived.at[1]),
    ]
    for copy in copies:
        copy.start()
    for copy in copies:
        copy.wait()
    gain = jnp.broadcast_to(column(gain_row[...]), (C, W))
    wide[...] = features[...].astype(F32)
    for frame in range(4):
        for row in range(4):
            values = wide[pl.ds(frame * 4 + row, C, stride=16), :]
            result = activation(values, gain).astype(BF16)
            act[frame, natural(row)] = result


def weight_kernel(first, second, first_bias, second_gain, second_bias, features, *targets):
    columns, kept = targets[-2:]
    kept[...] = features[...]
    for step, row in enumerate((first_bias, second_gain, second_bias)):
        columns[step] = jnp.broadcast_to(column(row[...]), (C, W))
    reversed_rows = lax.rem(lax.axis_index("height"), 2) == 1

    def arrange(mirrored):
        for source, (whole, late, last) in ((first, targets[0:3]), (second, targets[3:6])):
            for row_tap in range(3):
                for time_tap in range(3):
                    place = (row_tap * 3 + time_tap) * C
                    source_row = 2 - row_tap if mirrored else row_tap
                    for tap in range(3):
                        offset = ((time_tap * 3 + source_row) * 3 + tap) * C
                        block = source[:, offset : offset + C]
                        lines = slice(tap * C, (tap + 1) * C)
                        whole[lines, place : place + C] = block
                        if row_tap >= 1:
                            late[lines, place - 3 * C : place - 2 * C] = block
                        if row_tap == 2:
                            last[lines, place - 6 * C : place - 5 * C] = block

    pl.when(reversed_rows)(lambda: arrange(True))
    pl.when(jnp.logical_not(reversed_rows))(lambda: arrange(False))


def products(weight, left, right):
    stacked = jnp.concatenate([jnp.concatenate(left, axis=0), jnp.concatenate(right, axis=0)], axis=1)
    sums = jnp.dot(weight, stacked, preferred_element_type=F32)
    lane = lax.broadcasted_iota(jnp.int32, (C, W), 1)
    results = []
    for half in range(2):
        part = sums[:, half * W : (half + 1) * W]
        before = jnp.where(lane == 0, 0.0, pltpu.roll(part[:C], 1, 1))
        after = jnp.where(lane == W - 1, 0.0, pltpu.roll(part[2 * C :], W - 1, 1))
        results.append(part[C : 2 * C] + before + after)
    return results


def window(cell, frame, rows):
    return [cell(frame + step, row) for row in rows for step in range(3)]


def borders():
    height = lax.axis_index("height")
    outer = jnp.logical_or(height == 0, height == lax.axis_size("height") - 1)
    return lax.axis_index("tm") > 0, jnp.logical_not(outer)


def near_kernel(own, earlier, even, first_weight, second_weight, columns, near_hidden, branch_out, hidden):
    started, _ = borders()
    bias, gain, last_bias = columns[0], columns[1], columns[2]
    partner = 1 - lax.rem(lax.axis_index("height"), 2)

    def act(frame, row):
        if row > 3:
            return even[partner, frame, 5 - row]
        return earlier[frame, row] if frame < 4 else own[frame - 4, row]

    def inner(frame, row):
        return hidden[frame, row - 1]

    for frame in range(6):
        for row in (1, 3):
            pair = products(
                first_weight[...], window(act, frame, range(row - 1, row + 2)), window(act, frame, range(row, row + 3))
            )
            for step, sums in enumerate(pair):
                result = activation(sums + bias, gain)
                if frame < 2:
                    result = jnp.where(started, result, 0.0)
                hidden[frame, row - 1 + step] = result.astype(BF16)
                if row == 1:
                    near_hidden[frame, step] = result.astype(BF16)
    for frame in range(4):
        pair = products(
            second_weight[...], window(inner, frame, range(1, 4)), window(inner, frame, range(2, 5))
        )
        for step, sums in enumerate(pair):
            branch_out[frame, step] = sums + last_bias


def partial_kernel(
    own, earlier, far, near_hidden, first_weight, first_late, first_last, second_late, second_last, columns,
    far_hidden, first_part, branch_part,
):
    _, joined = borders()
    bias, gain, last_bias = columns[0], columns[1], columns[2]

    def act(frame, row):
        if row < 0:
            return far[frame - 4, -1 - row]
        return earlier[frame, row] if frame < 4 else own[frame - 4, row]

    def inner(frame, row):
        return near_hidden[frame, row - 1]

    for frame in (4, 5):
        pair = products(first_weight[...], window(act, frame, (-2, -1, 0)), window(act, frame, (-1, 0, 1)))
        for step, sums in enumerate(pair):
            result = activation(sums + bias, gain)
            if step == 0:
                result = jnp.where(joined, result, 0.0)
            far_hidden[frame - 4, step] = result.astype(BF16)
    for frame in (0, 2):
        for part, cell, base, weights, row in (
            (first_part, act, bias, (first_last, first_late), 0),
            (branch_part, inner, last_bias, (second_last, second_late), 1),
        ):
            for step, weight in enumerate(weights):
                rows = (row,) if step == 0 else (row, row + 1)
                pair = products(weight[...], window(cell, frame, rows), window(cell, frame + 1, rows))
                for later, sums in enumerate(pair):
                    part[frame + later, step] = sums + base


def far_kernel(
    features, far, corner, second_corner, third_corner, far_hidden, near_branch, first_part, branch_part, first_weight, second_weight, columns,
    encoded, hidden, total,
):
    started, joined = borders()
    gain = columns[1]

    def act(frame, row):
        if frame < 4:
            return corner[frame, -1 - row] + second_corner[frame, -1 - row] + third_corner[frame, -1 - row]
        return far[frame - 4, -1 - row]

    def outer(frame, row):
        return hidden[frame, row + 1] if frame < 4 else far_hidden[frame - 4, row + 1]

    for frame in (0, 2):
        for step, rows in ((0, (-2, -1)), (1, (-1,))):
            weight = first_weight[:, : len(rows) * 3 * C]
            pair = products(weight, window(act, frame, rows), window(act, frame + 1, rows))
            for later, sums in enumerate(pair):
                result = activation(sums + first_part[frame + later, step], gain)
                keep = None
                if frame == 0:
                    keep = jnp.logical_and(started, joined) if step == 0 else started
                elif step == 0:
                    keep = joined
                if keep is not None:
                    result = jnp.where(keep, result, 0.0)
                hidden[frame + later, step] = result.astype(BF16)
    for frame in range(4):
        for step in range(2):
            total[pl.ds(frame * 4 + natural(step + 2), C, stride=16), :] = near_branch[frame, step]
    for frame in (0, 2):
        for step, rows in ((0, (-1, 0)), (1, (0,))):
            weight = second_weight[:, : len(rows) * 3 * C]
            pair = products(weight, window(outer, frame, rows), window(outer, frame + 1, rows))
            for later, sums in enumerate(pair):
                place = (frame + later) * 4 + natural(step)
                total[pl.ds(place, C, stride=16), :] = sums + branch_part[frame + later, step]

    encoded[...] = (features[...].astype(F32) + total[...]).astype(BF16)


def shape(*dims, dtype=BF16):
    return jax.ShapeDtypeStruct(dims, dtype)


def call(kernel, out_shape, scratch, inputs, **kwargs):
    many = isinstance(out_shape, (list, tuple))
    return pl.pallas_call(
        kernel,
        out_shape=out_shape,
        in_specs=[VMEM] * len(inputs),
        out_specs=[VMEM] * len(out_shape) if many else VMEM,
        scratch_shapes=scratch,
        compiler_params=PARAMS,
        **kwargs,
    )(*inputs)


def held(array, flops, *others):
    return pl.pallas_call(
        lambda *refs: None,
        out_shape=shape(*array.shape),
        in_specs=[pl.BlockSpec(memory_space=pl.ANY)] * (1 + len(others)),
        out_specs=pl.BlockSpec(memory_space=pl.ANY),
        input_output_aliases={0: 0},
        compiler_params=pltpu.CompilerParams(vmem_limit_bytes=1 << 20),
        cost_estimate=pl.CostEstimate(flops=flops, bytes_accessed=0, transcendentals=0),
    )(array, *others)


def swap_pairs(first, count):
    edges = [(i, i + 1) for i in range(first, count - 1, 2)]
    return edges + [(b, a) for a, b in edges]


def routes(times, height):
    middle = (height // 2 - 1, height // 2)
    crossing, corner = [[], [], []], [[], [], []]
    for time in range(times):
        for a, b in swap_pairs(1, height):
            turn = TURNS.get(time, 0) if a in middle and b in middle else 0
            crossing[turn].append((time * height + a, time * height + b))
        for place in range(height):
            turn = TURNS.get(time, 0) if place in middle else 0
            if time + 1 < times:
                corner[turn].append((time * height + place, (time + 1) * height + place))
    return crossing, corner


def local(features, first_gain, first_weight, first_bias, second_gain, second_weight, second_bias):
    height, times = lax.axis_size("height"), lax.axis_size("tm")
    later = [(i, i + 1) for i in range(times - 1)]
    flat = features.reshape(C * 16, W)
    rows = [v.reshape(1, C) for v in (first_bias, second_gain, second_bias)]

    act = pl.pallas_call(
        first_act_kernel,
        out_shape=shape(4, 4, C, W),
        in_specs=[pl.BlockSpec(memory_space=pltpu.HBM)] * 2,
        out_specs=VMEM,
        scratch_shapes=[
            pltpu.VMEM((C * 16, W), BF16), pltpu.VMEM((1, C), F32), pltpu.VMEM((C * 16, W), F32),
            pltpu.SemaphoreType.DMA((2,)),
        ],
        compiler_params=PARAMS,
    )(*(pltpu.with_memory_space_constraint(v, pltpu.HBM) for v in (flat, first_gain.reshape(1, C))))
    edge = act[:, 0:2]
    crossing, corner = routes(times, height)
    fars = [lax.ppermute(edge, ("tm", "height"), pairs) for pairs in crossing]
    prepared = call(
        weight_kernel,
        [shape(3 * C, width * C) for width in (9, 6, 3)] * 2 + [shape(3, C, W, dtype=F32), shape(C * 16, W)], [],
        (first_weight, second_weight, *rows, flat),
        cost_estimate=pl.CostEstimate(flops=1 << 27, bytes_accessed=1 << 21, transcendentals=0),
    )
    first, first_late, first_last, second, second_late, second_last, columns, kept = prepared
    earlier = lax.ppermute(act, "tm", later)
    both = jnp.concatenate([earlier[:, 2:4], act[:, 2:4]], axis=0)
    even = lax.all_gather(both, "height", axis_index_groups=[[i, i + 1] for i in range(0, height, 2)])
    near_hidden, near_branch = call(
        near_kernel, [shape(6, 2, C, W), shape(4, 2, C, W, dtype=F32)], [pltpu.VMEM((6, 4, C, W), BF16)],
        (act, earlier, even, first, second, columns),
        cost_estimate=pl.CostEstimate(flops=1 << 20, bytes_accessed=1 << 10, transcendentals=0),
    )
    fars[0], fars[1] = (held(far, 1 << 33, near_hidden) for far in fars[:2])
    fars[2] = held(fars[2], 1 << 33, near_hidden, fars[1])
    corners = [lax.ppermute(far, ("tm", "height"), pairs) for far, pairs in zip(fars, corner)]
    corners[0] = held(corners[0], 1 << 28)
    far = fars[0] + fars[2] + fars[1]
    far_hidden, first_part, branch_part = call(
        partial_kernel,
        [shape(2, 2, C, W), shape(4, 2, C, W, dtype=F32), shape(4, 2, C, W, dtype=F32)], [],
        (act, earlier, far, near_hidden, first, first_late, first_last, second_late, second_last, columns),
        cost_estimate=pl.CostEstimate(flops=1 << 30, bytes_accessed=1 << 21, transcendentals=0),
    )
    encoded = call(
        far_kernel, shape(C * 16, W),
        [pltpu.VMEM((4, 2, C, W), BF16), pltpu.VMEM((C * 16, W), F32)],
        (kept, far, *corners, far_hidden, near_branch, first_part, branch_part, first, second, columns),
        cost_estimate=pl.CostEstimate(flops=8 * W * C * TAPS * 6, bytes_accessed=1 << 21, transcendentals=0),
    )
    return encoded.reshape(features.shape)


def solution(mesh):
    return jax.shard_map(
        local,
        mesh=mesh,
        in_specs=(P(None, "tm", "height", None), P(), P(), P(), P(), P(), P()),
        out_specs=P(None, "tm", "height", None),
        check_vma=False,
    )
```

```python
import functools

import jax
import jax.numpy as jnp
from jax import lax
from jax.experimental import pallas as pl
from jax.experimental.pallas import tpu as pltpu
from jax.sharding import PartitionSpec as P

C = 96
W = 128
TAPS = 9 * C
TURNS = {1: 1, 3: 1, 6: 1, 4: 2}
BF16 = jnp.bfloat16
F32 = jnp.float32
VMEM = pl.BlockSpec(memory_space=pltpu.VMEM)
PARAMS = pltpu.CompilerParams(vmem_limit_bytes=24 * 1024 * 1024)


def column(row):
    here = lax.broadcasted_iota(jnp.int32, (C, C), 0) == lax.broadcasted_iota(jnp.int32, (C, C), 1)
    return jnp.sum(jnp.where(here, row, 0.0), axis=1, keepdims=True)


def activation(values, gain):
    mean_square = jnp.sum(values * values, axis=0, keepdims=True) * (1.0 / C)
    scaled = values * lax.rsqrt(mean_square + 1e-06) * gain
    half = 0.5 * scaled
    return half + half * jnp.tanh(half)


def natural(row):
    return row + lax.rem(lax.axis_index("height"), 2) * (3 - 2 * row)


def first_act_kernel(features_in, gain_in, act, features, gain_row, wide, arrived):
    copies = [
        pltpu.make_async_copy(features_in, features, arrived.at[0]),
        pltpu.make_async_copy(gain_in, gain_row, arrived.at[1]),
    ]
    for copy in copies:
        copy.start()
    for copy in copies:
        copy.wait()
    gain = jnp.broadcast_to(column(gain_row[...]), (C, W))
    wide[...] = features[...].astype(F32)
    for frame in range(4):
        for row in range(4):
            values = wide[pl.ds(frame * 4 + row, C, stride=16), :]
            result = activation(values, gain).astype(BF16)
            act[frame, natural(row)] = result


def weight_kernel(first, second, first_bias, second_gain, second_bias, features, *targets):
    columns, kept = targets[-2:]
    kept[...] = features[...]
    for step, row in enumerate((first_bias, second_gain, second_bias)):
        columns[step] = jnp.broadcast_to(column(row[...]), (C, W))
    reversed_rows = lax.rem(lax.axis_index("height"), 2) == 1

    def arrange(mirrored):
        for source, (whole, late, last) in ((first, targets[0:3]), (second, targets[3:6])):
            for row_tap in range(3):
                for time_tap in range(3):
                    place = (row_tap * 3 + time_tap) * C
                    source_row = 2 - row_tap if mirrored else row_tap
                    for tap in range(3):
                        offset = ((time_tap * 3 + source_row) * 3 + tap) * C
                        block = source[:, offset : offset + C]
                        lines = slice(tap * C, (tap + 1) * C)
                        whole[lines, place : place + C] = block
                        if row_tap >= 1:
                            late[lines, place - 3 * C : place - 2 * C] = block
                        if row_tap == 2:
                            last[lines, place - 6 * C : place - 5 * C] = block

    pl.when(reversed_rows)(lambda: arrange(True))
    pl.when(jnp.logical_not(reversed_rows))(lambda: arrange(False))


def products(weight, left, right):
    stacked = jnp.concatenate([jnp.concatenate(left, axis=0), jnp.concatenate(right, axis=0)], axis=1)
    sums = jnp.dot(weight, stacked, preferred_element_type=F32)
    lane = lax.broadcasted_iota(jnp.int32, (C, W), 1)
    results = []
    for half in range(2):
        part = sums[:, half * W : (half + 1) * W]
        before = jnp.where(lane == 0, 0.0, pltpu.roll(part[:C], 1, 1))
        after = jnp.where(lane == W - 1, 0.0, pltpu.roll(part[2 * C :], W - 1, 1))
        results.append(part[C : 2 * C] + before + after)
    return results


def window(cell, frame, rows):
    return [cell(frame + step, row) for row in rows for step in range(3)]


def borders():
    height = lax.axis_index("height")
    outer = jnp.logical_or(height == 0, height == lax.axis_size("height") - 1)
    return lax.axis_index("tm") > 0, jnp.logical_not(outer)


def near_kernel(features, own, earlier, even, first_weight, second_weight, columns, near_hidden, base, hidden):
    base[...] = features[...].astype(F32)
    started, _ = borders()
    bias, gain, last_bias = columns[0], columns[1], columns[2]
    partner = 1 - lax.rem(lax.axis_index("height"), 2)

    def act(frame, row):
        if row > 3:
            return even[partner, frame, 5 - row]
        return earlier[frame, row] if frame < 4 else own[frame - 4, row]

    def inner(frame, row):
        return hidden[frame, row - 1]

    for frame in range(6):
        for row in (1, 3):
            pair = products(
                first_weight[...], window(act, frame, range(row - 1, row + 2)), window(act, frame, range(row, row + 3))
            )
            for step, sums in enumerate(pair):
                result = activation(sums + bias, gain)
                if frame < 2:
                    result = jnp.where(started, result, 0.0)
                hidden[frame, row - 1 + step] = result.astype(BF16)
                if row == 1:
                    near_hidden[frame, step] = result.astype(BF16)
    for frame in range(4):
        pair = products(
            second_weight[...], window(inner, frame, range(1, 4)), window(inner, frame, range(2, 5))
        )
        for step, sums in enumerate(pair):
            lines = pl.ds(frame * 4 + natural(step + 2), C, stride=16)
            base[lines, :] = base[lines, :] + (sums + last_bias)


def partial_kernel(
    own, earlier, far, near_hidden, first_weight, first_late, first_last, second_late, second_last, columns,
    far_hidden, first_part, branch_part,
):
    _, joined = borders()
    bias, gain, last_bias = columns[0], columns[1], columns[2]

    def act(frame, row):
        if row < 0:
            return far[frame - 4, -1 - row]
        return earlier[frame, row] if frame < 4 else own[frame - 4, row]

    def inner(frame, row):
        return near_hidden[frame, row - 1]

    for frame in (4, 5):
        pair = products(first_weight[...], window(act, frame, (-2, -1, 0)), window(act, frame, (-1, 0, 1)))
        for step, sums in enumerate(pair):
            result = activation(sums + bias, gain)
            if step == 0:
                result = jnp.where(joined, result, 0.0)
            far_hidden[frame - 4, step] = result.astype(BF16)
    for frame in (0, 2):
        for part, cell, base, weights, row in (
            (first_part, act, bias, (first_last, first_late), 0),
            (branch_part, inner, last_bias, (second_last, second_late), 1),
        ):
            for step, weight in enumerate(weights):
                rows = (row,) if step == 0 else (row, row + 1)
                pair = products(weight[...], window(cell, frame, rows), window(cell, frame + 1, rows))
                for later, sums in enumerate(pair):
                    part[frame + later, step] = sums + base


def far_kernel(
    base, far, corner, second_corner, third_corner, far_hidden, first_part, branch_part, first_weight, second_weight, columns,
    encoded, hidden, total,
):
    started, joined = borders()
    gain = columns[1]

    def act(frame, row):
        if frame < 4:
            return corner[frame, -1 - row] + second_corner[frame, -1 - row] + third_corner[frame, -1 - row]
        return far[frame - 4, -1 - row]

    def outer(frame, row):
        return hidden[frame, row + 1] if frame < 4 else far_hidden[frame - 4, row + 1]

    for frame in (0, 2):
        for step, rows in ((0, (-2, -1)), (1, (-1,))):
            weight = first_weight[:, : len(rows) * 3 * C]
            pair = products(weight, window(act, frame, rows), window(act, frame + 1, rows))
            for later, sums in enumerate(pair):
                result = activation(sums + first_part[frame + later, step], gain)
                keep = None
                if frame == 0:
                    keep = jnp.logical_and(started, joined) if step == 0 else started
                elif step == 0:
                    keep = joined
                if keep is not None:
                    result = jnp.where(keep, result, 0.0)
                hidden[frame + later, step] = result.astype(BF16)
    for frame in (0, 2):
        for step, rows in ((0, (-1, 0)), (1, (0,))):
            weight = second_weight[:, : len(rows) * 3 * C]
            pair = products(weight, window(outer, frame, rows), window(outer, frame + 1, rows))
            for later, sums in enumerate(pair):
                place = (frame + later) * 4 + natural(step)
                total[pl.ds(place, C, stride=16), :] = sums + branch_part[frame + later, step]

    low = lax.rem(lax.broadcasted_iota(jnp.int32, (C * 16, W), 0), 4) < 2
    even_place = lax.rem(lax.axis_index("height"), 2) == 0
    encoded[...] = (base[...] + jnp.where(low == even_place, total[...], 0.0)).astype(BF16)


def shape(*dims, dtype=BF16):
    return jax.ShapeDtypeStruct(dims, dtype)


def call(kernel, out_shape, scratch, inputs, **kwargs):
    many = isinstance(out_shape, (list, tuple))
    return pl.pallas_call(
        kernel,
        out_shape=out_shape,
        in_specs=[VMEM] * len(inputs),
        out_specs=[VMEM] * len(out_shape) if many else VMEM,
        scratch_shapes=scratch,
        compiler_params=PARAMS,
        **kwargs,
    )(*inputs)


def held(array, flops, *others):
    return pl.pallas_call(
        lambda *refs: None,
        out_shape=shape(*array.shape),
        in_specs=[pl.BlockSpec(memory_space=pl.ANY)] * (1 + len(others)),
        out_specs=pl.BlockSpec(memory_space=pl.ANY),
        input_output_aliases={0: 0},
        compiler_params=pltpu.CompilerParams(vmem_limit_bytes=1 << 20),
        cost_estimate=pl.CostEstimate(flops=flops, bytes_accessed=0, transcendentals=0),
    )(array, *others)


def swap_pairs(first, count):
    edges = [(i, i + 1) for i in range(first, count - 1, 2)]
    return edges + [(b, a) for a, b in edges]


def routes(times, height):
    middle = (height // 2 - 1, height // 2)
    crossing, corner = [[], [], []], [[], [], []]
    for time in range(times):
        for a, b in swap_pairs(1, height):
            turn = TURNS.get(time, 0) if a in middle and b in middle else 0
            crossing[turn].append((time * height + a, time * height + b))
        for place in range(height):
            turn = TURNS.get(time, 0) if place in middle else 0
            if time + 1 < times:
                corner[turn].append((time * height + place, (time + 1) * height + place))
    return crossing, corner


def local(features, first_gain, first_weight, first_bias, second_gain, second_weight, second_bias):
    height, times = lax.axis_size("height"), lax.axis_size("tm")
    later = [(i, i + 1) for i in range(times - 1)]
    flat = features.reshape(C * 16, W)
    rows = [v.reshape(1, C) for v in (first_bias, second_gain, second_bias)]

    act = pl.pallas_call(
        first_act_kernel,
        out_shape=shape(4, 4, C, W),
        in_specs=[pl.BlockSpec(memory_space=pltpu.HBM)] * 2,
        out_specs=VMEM,
        scratch_shapes=[
            pltpu.VMEM((C * 16, W), BF16), pltpu.VMEM((1, C), F32), pltpu.VMEM((C * 16, W), F32),
            pltpu.SemaphoreType.DMA((2,)),
        ],
        compiler_params=PARAMS,
    )(*(pltpu.with_memory_space_constraint(v, pltpu.HBM) for v in (flat, first_gain.reshape(1, C))))
    edge = act[:, 0:2]
    crossing, corner = routes(times, height)
    fars = [lax.ppermute(edge, ("tm", "height"), pairs) for pairs in crossing]
    prepared = call(
        weight_kernel,
        [shape(3 * C, width * C) for width in (9, 6, 3)] * 2 + [shape(3, C, W, dtype=F32), shape(C * 16, W)], [],
        (first_weight, second_weight, *rows, flat),
        cost_estimate=pl.CostEstimate(flops=1 << 27, bytes_accessed=1 << 21, transcendentals=0),
    )
    first, first_late, first_last, second, second_late, second_last, columns, kept = prepared
    earlier = lax.ppermute(act, "tm", later)
    both = jnp.concatenate([earlier[:, 2:4], act[:, 2:4]], axis=0)
    even = lax.all_gather(both, "height", axis_index_groups=[[i, i + 1] for i in range(0, height, 2)])
    near_hidden, base = call(
        near_kernel, [shape(6, 2, C, W), shape(C * 16, W, dtype=F32)], [pltpu.VMEM((6, 4, C, W), BF16)],
        (kept, act, earlier, even, first, second, columns),
        cost_estimate=pl.CostEstimate(flops=1 << 20, bytes_accessed=1 << 10, transcendentals=0),
    )
    fars[0], fars[1] = (held(far, 1 << 33, near_hidden) for far in fars[:2])
    fars[2] = held(fars[2], 1 << 33, near_hidden, fars[1])
    corners = [lax.ppermute(far, ("tm", "height"), pairs) for far, pairs in zip(fars, corner)]
    corners[0] = held(corners[0], 1 << 28)
    far = fars[0] + fars[2] + fars[1]
    far_hidden, first_part, branch_part = call(
        partial_kernel,
        [shape(2, 2, C, W), shape(4, 2, C, W, dtype=F32), shape(4, 2, C, W, dtype=F32)], [],
        (act, earlier, far, near_hidden, first, first_late, first_last, second_late, second_last, columns),
        cost_estimate=pl.CostEstimate(flops=1 << 30, bytes_accessed=1 << 21, transcendentals=0),
    )
    encoded = call(
        far_kernel, shape(C * 16, W),
        [pltpu.VMEM((4, 2, C, W), BF16), pltpu.VMEM((C * 16, W), F32)],
        (base, far, *corners, far_hidden, first_part, branch_part, first, second, columns),
        cost_estimate=pl.CostEstimate(flops=8 * W * C * TAPS * 6, bytes_accessed=1 << 21, transcendentals=0),
    )
    return encoded.reshape(features.shape)


def solution(mesh):
    return jax.shard_map(
        local,
        mesh=mesh,
        in_specs=(P(None, "tm", "height", None), P(), P(), P(), P(), P(), P()),
        out_specs=P(None, "tm", "height", None),
        check_vma=False,
    )
```

```python
import functools

import jax
import jax.numpy as jnp
from jax import lax
from jax.experimental import pallas as pl
from jax.experimental.pallas import tpu as pltpu
from jax.sharding import PartitionSpec as P

C = 96
W = 128
TAPS = 9 * C
TURNS = {1: 1, 3: 1, 4: 1, 6: 1}
BF16 = jnp.bfloat16
F32 = jnp.float32
VMEM = pl.BlockSpec(memory_space=pltpu.VMEM)
PARAMS = pltpu.CompilerParams(vmem_limit_bytes=24 * 1024 * 1024)


def column(row):
    here = lax.broadcasted_iota(jnp.int32, (C, C), 0) == lax.broadcasted_iota(jnp.int32, (C, C), 1)
    return jnp.sum(jnp.where(here, row, 0.0), axis=1, keepdims=True)


def activation(values, gain):
    mean_square = jnp.sum(values * values, axis=0, keepdims=True) * (1.0 / C)
    scaled = values * lax.rsqrt(mean_square + 1e-06) * gain
    half = 0.5 * scaled
    return half + half * jnp.tanh(half)


def natural(row):
    return row + lax.rem(lax.axis_index("height"), 2) * (3 - 2 * row)


def first_act_kernel(features_in, gain_in, act, features, gain_row, wide, arrived):
    copies = [
        pltpu.make_async_copy(features_in, features, arrived.at[0]),
        pltpu.make_async_copy(gain_in, gain_row, arrived.at[1]),
    ]
    for copy in copies:
        copy.start()
    for copy in copies:
        copy.wait()
    gain = jnp.broadcast_to(column(gain_row[...]), (C, W))
    wide[...] = features[...].astype(F32)
    for frame in range(4):
        for row in range(4):
            values = wide[pl.ds(frame * 4 + row, C, stride=16), :]
            result = activation(values, gain).astype(BF16)
            act[frame, natural(row)] = result


def weight_kernel(first, second, first_bias, second_gain, second_bias, features, *targets):
    columns, kept = targets[-2:]
    kept[...] = features[...]
    for step, row in enumerate((first_bias, second_gain, second_bias)):
        columns[step] = jnp.broadcast_to(column(row[...]), (C, W))
    reversed_rows = lax.rem(lax.axis_index("height"), 2) == 1

    def arrange(mirrored):
        for source, (whole, late, last) in ((first, targets[0:3]), (second, targets[3:6])):
            for row_tap in range(3):
                for time_tap in range(3):
                    place = (row_tap * 3 + time_tap) * C
                    source_row = 2 - row_tap if mirrored else row_tap
                    for tap in range(3):
                        offset = ((time_tap * 3 + source_row) * 3 + tap) * C
                        block = source[:, offset : offset + C]
                        lines = slice(tap * C, (tap + 1) * C)
                        whole[lines, place : place + C] = block
                        if row_tap >= 1:
                            late[lines, place - 3 * C : place - 2 * C] = block
                        if row_tap == 2:
                            last[lines, place - 6 * C : place - 5 * C] = block

    pl.when(reversed_rows)(lambda: arrange(True))
    pl.when(jnp.logical_not(reversed_rows))(lambda: arrange(False))


def products(weight, left, right):
    stacked = jnp.concatenate([jnp.concatenate(left, axis=0), jnp.concatenate(right, axis=0)], axis=1)
    sums = jnp.dot(weight, stacked, preferred_element_type=F32)
    lane = lax.broadcasted_iota(jnp.int32, (C, W), 1)
    results = []
    for half in range(2):
        part = sums[:, half * W : (half + 1) * W]
        before = jnp.where(lane == 0, 0.0, pltpu.roll(part[:C], 1, 1))
        after = jnp.where(lane == W - 1, 0.0, pltpu.roll(part[2 * C :], W - 1, 1))
        results.append(part[C : 2 * C] + before + after)
    return results


def window(cell, frame, rows):
    return [cell(frame + step, row) for row in rows for step in range(3)]


def borders():
    height = lax.axis_index("height")
    outer = jnp.logical_or(height == 0, height == lax.axis_size("height") - 1)
    return lax.axis_index("tm") > 0, jnp.logical_not(outer)


def near_kernel(features, own, earlier, even, first_weight, second_weight, columns, near_hidden, base, hidden):
    base[...] = features[...].astype(F32)
    started, _ = borders()
    bias, gain, last_bias = columns[0], columns[1], columns[2]
    partner = 1 - lax.rem(lax.axis_index("height"), 2)

    def act(frame, row):
        if row > 3:
            return even[partner, frame, 5 - row]
        return earlier[frame, row] if frame < 4 else own[frame - 4, row]

    def inner(frame, row):
        return hidden[frame, row - 1]

    for frame in range(6):
        for row in (1, 3):
            pair = products(
                first_weight[...], window(act, frame, range(row - 1, row + 2)), window(act, frame, range(row, row + 3))
            )
            for step, sums in enumerate(pair):
                result = activation(sums + bias, gain)
                if frame < 2:
                    result = jnp.where(started, result, 0.0)
                hidden[frame, row - 1 + step] = result.astype(BF16)
                if row == 1:
                    near_hidden[frame, step] = result.astype(BF16)
    for frame in range(4):
        pair = products(
            second_weight[...], window(inner, frame, range(1, 4)), window(inner, frame, range(2, 5))
        )
        for step, sums in enumerate(pair):
            lines = pl.ds(frame * 4 + natural(step + 2), C, stride=16)
            base[lines, :] = base[lines, :] + (sums + last_bias)


def partial_kernel(
    own, earlier, far, near_hidden, first_weight, first_late, first_last, second_late, second_last, columns,
    far_hidden, first_part, branch_part,
):
    _, joined = borders()
    bias, gain, last_bias = columns[0], columns[1], columns[2]

    def act(frame, row):
        if row < 0:
            return far[frame - 4, -1 - row]
        return earlier[frame, row] if frame < 4 else own[frame - 4, row]

    def inner(frame, row):
        return near_hidden[frame, row - 1]

    for frame in (4, 5):
        pair = products(first_weight[...], window(act, frame, (-2, -1, 0)), window(act, frame, (-1, 0, 1)))
        for step, sums in enumerate(pair):
            result = activation(sums + bias, gain)
            if step == 0:
                result = jnp.where(joined, result, 0.0)
            far_hidden[frame - 4, step] = result.astype(BF16)
    for frame in (0, 2):
        for part, cell, base, weights, row in (
            (first_part, act, bias, (first_last, first_late), 0),
            (branch_part, inner, last_bias, (second_last, second_late), 1),
        ):
            for step, weight in enumerate(weights):
                rows = (row,) if step == 0 else (row, row + 1)
                pair = products(weight[...], window(cell, frame, rows), window(cell, frame + 1, rows))
                for later, sums in enumerate(pair):
                    part[frame + later, step] = sums + base


def far_kernel(
    base, far, corner, second_corner, far_hidden, first_part, branch_part, first_weight, second_weight, columns,
    encoded, hidden, total,
):
    started, joined = borders()
    gain = columns[1]

    def act(frame, row):
        if frame < 4:
            return corner[frame, -1 - row] + second_corner[frame, -1 - row]
        return far[frame - 4, -1 - row]

    def outer(frame, row):
        return hidden[frame, row + 1] if frame < 4 else far_hidden[frame - 4, row + 1]

    for frame in (0, 2):
        for step, rows in ((0, (-2, -1)), (1, (-1,))):
            weight = first_weight[:, : len(rows) * 3 * C]
            pair = products(weight, window(act, frame, rows), window(act, frame + 1, rows))
            for later, sums in enumerate(pair):
                result = activation(sums + first_part[frame + later, step], gain)
                keep = None
                if frame == 0:
                    keep = jnp.logical_and(started, joined) if step == 0 else started
                elif step == 0:
                    keep = joined
                if keep is not None:
                    result = jnp.where(keep, result, 0.0)
                hidden[frame + later, step] = result.astype(BF16)
    for frame in (0, 2):
        for step, rows in ((0, (-1, 0)), (1, (0,))):
            weight = second_weight[:, : len(rows) * 3 * C]
            pair = products(weight, window(outer, frame, rows), window(outer, frame + 1, rows))
            for later, sums in enumerate(pair):
                place = (frame + later) * 4 + natural(step)
                total[pl.ds(place, C, stride=16), :] = sums + branch_part[frame + later, step]

    low = lax.rem(lax.broadcasted_iota(jnp.int32, (C * 16, W), 0), 4) < 2
    even_place = lax.rem(lax.axis_index("height"), 2) == 0
    encoded[...] = (base[...] + jnp.where(low == even_place, total[...], 0.0)).astype(BF16)


def shape(*dims, dtype=BF16):
    return jax.ShapeDtypeStruct(dims, dtype)


def call(kernel, out_shape, scratch, inputs, **kwargs):
    many = isinstance(out_shape, (list, tuple))
    return pl.pallas_call(
        kernel,
        out_shape=out_shape,
        in_specs=[VMEM] * len(inputs),
        out_specs=[VMEM] * len(out_shape) if many else VMEM,
        scratch_shapes=scratch,
        compiler_params=PARAMS,
        **kwargs,
    )(*inputs)


def held(array, flops, *others):
    return pl.pallas_call(
        lambda *refs: None,
        out_shape=shape(*array.shape),
        in_specs=[pl.BlockSpec(memory_space=pl.ANY)] * (1 + len(others)),
        out_specs=pl.BlockSpec(memory_space=pl.ANY),
        input_output_aliases={0: 0},
        compiler_params=pltpu.CompilerParams(vmem_limit_bytes=1 << 20),
        cost_estimate=pl.CostEstimate(flops=flops, bytes_accessed=0, transcendentals=0),
    )(array, *others)


def swap_pairs(first, count):
    edges = [(i, i + 1) for i in range(first, count - 1, 2)]
    return edges + [(b, a) for a, b in edges]


def routes(times, height):
    middle = (height // 2 - 1, height // 2)
    crossing, corner = [[], []], [[], []]
    for time in range(times):
        for a, b in swap_pairs(1, height):
            turn = TURNS.get(time, 0) if a in middle and b in middle else 0
            crossing[turn].append((time * height + a, time * height + b))
        for place in range(height):
            turn = TURNS.get(time, 0) if place in middle else 0
            if time + 1 < times:
                corner[turn].append((time * height + place, (time + 1) * height + place))
    return crossing, corner


def local(features, first_gain, first_weight, first_bias, second_gain, second_weight, second_bias):
    height, times = lax.axis_size("height"), lax.axis_size("tm")
    later = [(i, i + 1) for i in range(times - 1)]
    flat = features.reshape(C * 16, W)
    rows = [v.reshape(1, C) for v in (first_bias, second_gain, second_bias)]

    act = pl.pallas_call(
        first_act_kernel,
        out_shape=shape(4, 4, C, W),
        in_specs=[pl.BlockSpec(memory_space=pltpu.HBM)] * 2,
        out_specs=VMEM,
        scratch_shapes=[
            pltpu.VMEM((C * 16, W), BF16), pltpu.VMEM((1, C), F32), pltpu.VMEM((C * 16, W), F32),
            pltpu.SemaphoreType.DMA((2,)),
        ],
        compiler_params=PARAMS,
    )(*(pltpu.with_memory_space_constraint(v, pltpu.HBM) for v in (flat, first_gain.reshape(1, C))))
    edge = act[:, 0:2]
    crossing, corner = routes(times, height)
    fars = [lax.ppermute(edge, ("tm", "height"), pairs) for pairs in crossing]
    prepared = call(
        weight_kernel,
        [shape(3 * C, width * C) for width in (9, 6, 3)] * 2 + [shape(3, C, W, dtype=F32), shape(C * 16, W)], [],
        (first_weight, second_weight, *rows, flat),
        cost_estimate=pl.CostEstimate(flops=1 << 27, bytes_accessed=1 << 21, transcendentals=0),
    )
    first, first_late, first_last, second, second_late, second_last, columns, kept = prepared
    earlier = lax.ppermute(act, "tm", later)
    both = jnp.concatenate([earlier[:, 2:4], act[:, 2:4]], axis=0)
    even = lax.all_gather(both, "height", axis_index_groups=[[i, i + 1] for i in range(0, height, 2)])
    near_hidden, base = call(
        near_kernel, [shape(6, 2, C, W), shape(C * 16, W, dtype=F32)], [pltpu.VMEM((6, 4, C, W), BF16)],
        (kept, act, earlier, even, first, second, columns),
        cost_estimate=pl.CostEstimate(flops=1 << 20, bytes_accessed=1 << 10, transcendentals=0),
    )
    fars = [held(far, 1 << 33, near_hidden) for far in fars]
    corners = [lax.ppermute(far, ("tm", "height"), pairs) for far, pairs in zip(fars, corner)]
    corners[0] = held(corners[0], 1 << 28)
    far = fars[0] + fars[1]
    far_hidden, first_part, branch_part = call(
        partial_kernel,
        [shape(2, 2, C, W), shape(4, 2, C, W, dtype=F32), shape(4, 2, C, W, dtype=F32)], [],
        (act, earlier, far, near_hidden, first, first_late, first_last, second_late, second_last, columns),
        cost_estimate=pl.CostEstimate(flops=1 << 30, bytes_accessed=1 << 21, transcendentals=0),
    )
    encoded = call(
        far_kernel, shape(C * 16, W),
        [pltpu.VMEM((4, 2, C, W), BF16), pltpu.VMEM((C * 16, W), F32)],
        (base, far, *corners, far_hidden, first_part, branch_part, first, second, columns),
        cost_estimate=pl.CostEstimate(flops=8 * W * C * TAPS * 6, bytes_accessed=1 << 21, transcendentals=0),
    )
    return encoded.reshape(features.shape)


def solution(mesh):
    return jax.shard_map(
        local,
        mesh=mesh,
        in_specs=(P(None, "tm", "height", None), P(), P(), P(), P(), P(), P()),
        out_specs=P(None, "tm", "height", None),
        check_vma=False,
    )
```
